32 devices in a mesh: slab: 16 (over z, x, core), obs: 2 (over y).
Axes of the slice: x: 2, y: 2, z: 4, core: 2. Of those that a mesh axis runs over, the one named last changes fastest.
Arguments:
- background_members: float32 [64, 65536], P('slab', 'obs'), may hold values from -6 to 6
- measurement_jitter: bfloat16 [64, 2, 16384], P(None, 'obs', 'slab'), may hold values from -5 to 5
- measurement_readings: float32 [2, 16384], P('obs', 'slab'), may hold values from -8 to 8
- measurement_noise_spread: float32 [2, 16384], P('obs', 'slab'), may hold values from 0.2 to 2
- measurement_grid_location: int32 [2, 16384], P('obs', 'slab'), may hold values from 0 to 2047
- active_tallies: int32 [2, 16], P('obs', 'slab'), may hold values from 128 to 1024, as said below
- coupling_listing: int32 [2, 512, 8], P('obs', 'slab'), may hold values from 0 to 15, as said below
- taper_factors: float32 [2, 512, 8], P('obs', 'slab'), may hold values from 0.1 to 1
Outputs:
- analysis: float32 [64, 65536], P('slab', 'obs')
The draws below stay inside these ranges and needn't reach their ends.
Inputs may be any that keep to these rules, and one draw needn't show every extreme that they name: `active_tallies`: some region of some group holds 1024 live observations; slots beyond a region's count are padding. `coupling_listing`: the 8 observation blocks listed for a state block are distinct.
All inputs are finite; a program needn't handle non-finite values.
Results may differ from the reference program's by a relative error of at most 0.0063.
Values may be sent and summed in bfloat16 or wider, within the bound.
A program may use at most 64 MiB of HBM per device.

```python
import math
import jax
import jax.numpy as jnp
from jax import lax

MEMBER_TOTAL = 64
BS = 64
OB = 128
L = 8
NBD = 32
OBD = 8
GROUPS = 2
REGIONS = 16
SP = 2048
OBSD = 1024
SLABBLK = 512
SLABOBS = 16384
NOBG = 16
GRID_LOCATIONS = 65536


def draw_active_tallies(key, part):
    key_low, key_full = jax.random.split(key)
    values = jax.random.randint(key_low, (GROUPS * REGIONS,), OBSD // 8, OBSD + 1, dtype=jnp.int32)
    fullest = jax.random.randint(key_full, (), 0, GROUPS * REGIONS, dtype=jnp.int32)
    values = jnp.where(jnp.arange(GROUPS * REGIONS, dtype=jnp.int32) == fullest, OBSD, values)
    return values.reshape(GROUPS, REGIONS)


def pick_blocks(row_key):
    return jax.random.permutation(row_key, NOBG)[:L]


def draw_coupling_listing(key, part):
    row_keys = jax.random.split(key, GROUPS * SLABBLK)
    chosen = jax.vmap(pick_blocks)(row_keys)
    return chosen.astype(jnp.int32).reshape(GROUPS, SLABBLK, L)


def place_ends(result, key, smallest, top_value):
    longest = result.shape.index(max(result.shape))
    spots = []
    for shift in (0, 1):
        where = [jax.random.randint(jax.random.fold_in(key, axis), (), 0, length) for axis, length in enumerate(result.shape)]
        where[longest] = (where[longest] + shift) % result.shape[longest]
        spots.append(tuple(where))
    return result.at[spots[0]].set(smallest).at[spots[1]].set(top_value)


def level_of(key, dims, cuts, smallest, largest):
    factor_of, own = 1.0, jax.random.fold_in(key, 6)
    for dim, shards_of in cuts:
        heights = jnp.exp(jax.random.uniform(jax.random.fold_in(own, dim), (shards_of,), jnp.float32, smallest / len(cuts), largest / len(cuts)))
        factor_of = factor_of * jnp.repeat(heights, dims[dim] // shards_of).reshape([-1 if axis == dim else 1 for axis in range(len(dims))])
    return factor_of


def scatter_about(key, extent, scale, limit, cuts=(), held_as=jnp.bfloat16):
    entries = jax.random.normal(key, extent, jnp.float32) * scale
    if len(cuts) > 0:
        entries = level_of(key, extent, cuts, -0.22, 0.18) * entries
    return jnp.clip(entries, min=-limit, max=limit).astype(held_as)


def setup_inputs(seed: int = 0) -> dict:
    seeds = jax.random.split(jax.random.key(seed), 9)
    background_members = scatter_about(seeds[0], (MEMBER_TOTAL, GRID_LOCATIONS), 1.0, 6.0, ((0, 16), (1, 2)), jnp.float32)
    measurement_jitter = scatter_about(seeds[1], (MEMBER_TOTAL, GROUPS, SLABOBS), 1.0, 5.0, ((1, 2), (2, 16)))
    measurement_readings = scatter_about(seeds[2], (GROUPS, SLABOBS), 2.0, 8.0, ((0, 2), (1, 16)), jnp.float32)
    measurement_noise_spread = jnp.clip(jnp.exp(math.log(2.0) - 2.3025851 * jax.random.uniform(seeds[3], (GROUPS, SLABOBS), jnp.float32) ** level_of(seeds[3], (GROUPS, SLABOBS), ((0, 2), (1, 16)), -0.2, 0.2)), 0.2, 2.0)
    measurement_grid_location = place_ends(jax.random.randint(seeds[4], (GROUPS, SLABOBS), 0, SP), jax.random.fold_in(seeds[4], 1), 0, SP - 1).astype(jnp.int32)
    active_tallies = draw_active_tallies(jax.random.fold_in(seeds[8], 71), 0)
    coupling_listing = draw_coupling_listing(jax.random.fold_in(seeds[8], 71), 0)
    taper_factors = jnp.clip(jnp.exp(math.log(1.0) - 2.3025851 * jax.random.uniform(seeds[7], (GROUPS, SLABBLK, L), jnp.float32) ** level_of(seeds[7], (GROUPS, SLABBLK, L), ((0, 2), (1, 16)), -0.2, 0.2)), 0.1, 1.0)
    return {"background_members": background_members, "measurement_jitter": measurement_jitter, "measurement_readings": measurement_readings, "measurement_noise_spread": measurement_noise_spread, "measurement_grid_location": measurement_grid_location, "active_tallies": active_tallies, "coupling_listing": coupling_listing, "taper_factors": taper_factors}


def reference(background_members, measurement_jitter, measurement_readings, measurement_noise_spread, measurement_grid_location, active_tallies, coupling_listing, taper_factors):
    highest = lax.Precision.HIGHEST
    temporary_storage = lax.optimization_barrier(background_members.astype(jnp.bfloat16)).astype(jnp.float32)
    state_tiles = temporary_storage.reshape(MEMBER_TOTAL, GROUPS, REGIONS, SP)
    deviation = state_tiles - jnp.mean(state_tiles, axis=0, keepdims=True)
    obs_places = jnp.broadcast_to(measurement_grid_location.reshape(1, GROUPS, REGIONS, OBSD), (MEMBER_TOTAL, GROUPS, REGIONS, OBSD))
    prior_value = jnp.take_along_axis(state_tiles, obs_places, axis=3)
    prior_shift = prior_value - jnp.mean(prior_value, axis=0, keepdims=True)
    spread = jnp.sum(prior_shift * prior_shift, axis=0, keepdims=True) / (MEMBER_TOTAL - 1)
    values = measurement_readings.reshape(1, GROUPS, REGIONS, OBSD)
    errors = measurement_noise_spread.reshape(1, GROUPS, REGIONS, OBSD)
    obs_noise = measurement_jitter.reshape(MEMBER_TOTAL, GROUPS, REGIONS, OBSD).astype(jnp.float32)
    usable = jnp.arange(OBSD, dtype=jnp.int32)[None, None, None, :] < active_tallies[None, :, :, None]
    innovation = (values + obs_noise - prior_value) / (spread + errors)
    gain_input = jnp.where(usable, innovation, jnp.float32(0.0))
    gain_low = lax.optimization_barrier(gain_input.astype(jnp.bfloat16)).astype(jnp.float32)
    prior_low = lax.optimization_barrier(prior_shift.astype(jnp.bfloat16)).astype(jnp.float32)

    def per_region(region):
        region_prior = lax.dynamic_index_in_dim(prior_low, region, 2, keepdims=False).reshape(MEMBER_TOTAL, GROUPS * OBD, OB)
        region_gain = lax.dynamic_index_in_dim(gain_low, region, 2, keepdims=False).reshape(MEMBER_TOTAL, GROUPS * OBD, OB)
        products = jnp.einsum("mco,nco->cmn", region_gain, region_prior, precision=highest)
        region_links = lax.dynamic_slice_in_dim(coupling_listing, region * NBD, NBD, 1)
        factor = lax.dynamic_slice_in_dim(taper_factors, region * NBD, NBD, 1) / (MEMBER_TOTAL - 1)
        choose = region_links[..., None] == jnp.arange(GROUPS * OBD, dtype=jnp.int32)
        localize = jnp.sum(jnp.where(choose, factor[..., None], jnp.float32(0.0)), axis=2)
        ensemble = jnp.einsum("gbc,cmn->gbmn", localize, products, precision=highest)
        region_dev = lax.dynamic_index_in_dim(deviation, region, 2, keepdims=False).reshape(MEMBER_TOTAL, GROUPS, NBD, BS)
        return jnp.einsum("gbmn,ngbp->mgbp", ensemble, region_dev, precision=highest)

    increments = lax.map(per_region, jnp.arange(REGIONS, dtype=jnp.int32))
    increments = jnp.moveaxis(increments, 0, 2).reshape(MEMBER_TOTAL, GRID_LOCATIONS)
    reduced_correction = lax.optimization_barrier(increments.astype(jnp.bfloat16)).astype(jnp.float32)
    return background_members + reduced_correction
```

```python
import functools

import jax
import jax.numpy as jnp
from jax import lax
from jax.experimental import pallas as pl
from jax.experimental.pallas import tpu as pltpu
from jax.sharding import PartitionSpec as P

LANES = 128
MESH = pl.DeviceIdType.MESH


def kernel(
    slabs,
    groups,
    bg,
    jitter,
    readings,
    noise,
    location,
    tally,
    coupling,
    taper,
    out,
    rows_f32,
    send1,
    recv1,
    mem_f32,
    tiles,
    dev,
    shared,
    prod,
    inc_f32,
    send2,
    recv2,
    send1_sem,
    recv1_sem,
    sendp_sem,
    recvp_sem,
    send2_sem,
    recv2_sem,
):
    own = bg.shape[0]
    span = bg.shape[1] // slabs
    cols = span // LANES
    rows = own * cols
    members = own * slabs
    half = members // 2
    chunks = location.shape[1] // LANES
    links, blocks = coupling.shape
    me = lax.axis_index("slab")
    group = lax.axis_index("obs")

    barrier = pltpu.get_barrier_semaphore()

    @pl.loop(1, slabs)
    def _(k):
        pl.semaphore_signal(
            barrier, inc=1, device_id=(lax.rem(me + k, slabs), group), device_id_type=MESH
        )

    for k in range(1, groups):
        pl.semaphore_signal(
            barrier, inc=1, device_id=(me, lax.rem(group + k, groups)), device_id_type=MESH
        )

    @pl.loop(0, slabs)
    def _(s):
        for q in range(cols):
            part = bg[:, pl.ds(pl.multiple_of(s * span + q * LANES, LANES), LANES)]
            if own == 1:
                rows_f32[pl.ds(s * rows + q, 1), :] = part
            else:
                rows_f32[pl.ds(s * rows + q, own, stride=cols), :] = part
        send1[s] = rows_f32[pl.ds(pl.multiple_of(s * rows, 16), rows), :].astype(jnp.bfloat16)

    pl.semaphore_wait(barrier, slabs - 1 + groups - 1)

    def forward(k):
        to = lax.rem(me + k, slabs)
        return pltpu.make_async_remote_copy(
            src_ref=send1.at[to],
            dst_ref=recv1.at[me],
            send_sem=send1_sem.at[to],
            recv_sem=recv1_sem.at[me],
            device_id=(to, group),
            device_id_type=MESH,
        )

    def arrived(k):
        source = lax.rem(me - k + slabs, slabs)
        return source, pltpu.make_async_remote_copy(
            src_ref=send1.at[source],
            dst_ref=recv1.at[source],
            send_sem=send1_sem.at[source],
            recv_sem=recv1_sem.at[source],
            device_id=(source, group),
            device_id_type=MESH,
        )

    @pl.loop(1, slabs)
    def _(k):
        forward(k).start()

    mem_f32[pl.ds(pl.multiple_of(me * rows, 16), rows), :] = send1[me].astype(jnp.float32)

    @pl.loop(1, slabs)
    def _(k):
        source, copy = arrived(k)
        copy.wait_recv()
        mem_f32[pl.ds(pl.multiple_of(source * rows, 16), rows), :] = recv1[source].astype(
            jnp.float32
        )

    for q in range(cols):
        tile = mem_f32[pl.ds(q, members, stride=cols), :]
        tiles[q] = tile
        dev[q] = (tile - jnp.mean(tile, axis=0, keepdims=True)).astype(jnp.bfloat16)

    live = tally[0, 0]

    @pl.loop(0, chunks)
    def _(c):
        here = pl.ds(pl.multiple_of(c * LANES, LANES), LANES)
        place = location[:, here]
        column = jnp.broadcast_to(place // LANES, (members, LANES))
        lane = jnp.broadcast_to(place % LANES, (members, LANES))
        prior = jnp.zeros((members, LANES), jnp.float32)
        for q in range(cols):
            picked = jnp.take_along_axis(tiles[q], lane, axis=1, mode="promise_in_bounds")
            prior = jnp.where(column == q, picked, prior)
        shift = prior - jnp.mean(prior, axis=0, keepdims=True)
        spread = jnp.sum(shift * shift, axis=0, keepdims=True) / (members - 1)
        innovation = (readings[:, here] + jitter[:, here].astype(jnp.float32) - prior) / (
            spread + noise[:, here]
        )
        slot = c * LANES + lax.broadcasted_iota(jnp.int32, (members, LANES), 1)
        gain = jnp.where(slot < live, innovation, 0.0).astype(jnp.bfloat16)
        product = lax.dot_general(
            gain,
            shift.astype(jnp.bfloat16),
            (((1,), (1,)), ((), ())),
            preferred_element_type=jnp.float32,
        )
        packed = jnp.concatenate([product[:half], product[half:]], axis=1)
        prod[group * chunks + c] = packed
        shared[group, c] = packed.astype(jnp.bfloat16)

    for k in range(1, groups):
        to = lax.rem(group + k, groups)
        pltpu.make_async_remote_copy(
            src_ref=shared.at[group],
            dst_ref=shared.at[group],
            send_sem=sendp_sem.at[to],
            recv_sem=recvp_sem.at[group],
            device_id=(me, to),
            device_id_type=MESH,
        ).start()
    for k in range(1, groups):
        source = lax.rem(group + k, groups)
        pltpu.make_async_remote_copy(
            src_ref=shared.at[source],
            dst_ref=shared.at[source],
            send_sem=sendp_sem.at[source],
            recv_sem=recvp_sem.at[source],
            device_id=(me, source),
            device_id_type=MESH,
        ).wait_recv()
        for c in range(chunks):
            prod[source * chunks + c] = shared[source, c].astype(jnp.float32)

    low_lane = lax.broadcasted_iota(jnp.int32, (2 * half, LANES), 1) < LANES // 2
    low_half = lax.broadcasted_iota(jnp.int32, (half, LANES), 1) < LANES // 2

    @pl.loop(0, cols)
    def _(q):
        parts = []
        for h in range(2):
            b = 2 * q + h
            total = taper[0, b] * prod[coupling[0, b]]
            for l in range(1, links):
                total = total + taper[l, b] * prod[coupling[l, b]]
            parts.append(total * (1.0 / (members - 1)))
        pair = jnp.concatenate(parts, axis=0)
        left = jnp.concatenate(
            [jnp.where(low_lane, pair, 0.0), jnp.where(low_lane, 0.0, pair)], axis=0
        ).astype(jnp.bfloat16)
        right = dev[q]
        right = jnp.concatenate([right, right], axis=0)
        update = jnp.dot(left, right, preferred_element_type=jnp.float32)
        inc_f32[pl.ds(q, half, stride=cols), :] = jnp.where(
            low_half, update[:half], update[half : 2 * half]
        )
        inc_f32[pl.ds(q + half * cols, half, stride=cols), :] = jnp.where(
            low_half, update[2 * half : 3 * half], update[3 * half :]
        )

    def backward(to):
        return pltpu.make_async_remote_copy(
            src_ref=send2.at[to],
            dst_ref=recv2.at[me],
            send_sem=send2_sem.at[to],
            recv_sem=recv2_sem.at[me],
            device_id=(to, group),
            device_id_type=MESH,
        )

    def back(source):
        return pltpu.make_async_remote_copy(
            src_ref=send2.at[source],
            dst_ref=recv2.at[source],
            send_sem=send2_sem.at[source],
            recv_sem=recv2_sem.at[source],
            device_id=(source, group),
            device_id_type=MESH,
        )

    @pl.loop(1, slabs)
    def _(k):
        to = lax.rem(me + k, slabs)
        send2[to] = inc_f32[pl.ds(pl.multiple_of(to * rows, 16), rows), :].astype(jnp.bfloat16)
        backward(to).start()

    def finish(s, low):
        rows_f32[pl.ds(pl.multiple_of(s * rows, 16), rows), :] = low.astype(jnp.float32)
        for q in range(cols):
            at = pl.ds(pl.multiple_of(s * span + q * LANES, LANES), LANES)
            if own == 1:
                part = rows_f32[pl.ds(s * rows + q, 1), :]
            else:
                part = rows_f32[pl.ds(s * rows + q, own, stride=cols), :]
            out[:, at] = bg[:, at] + part

    finish(me, inc_f32[pl.ds(pl.multiple_of(me * rows, 16), rows), :].astype(jnp.bfloat16))

    @pl.loop(1, slabs)
    def _(k):
        source = lax.rem(me - k + slabs, slabs)
        back(source).wait_recv()
        finish(source, recv2[source])

    @pl.loop(1, slabs)
    def _(k):
        forward(k).wait_send()
        backward(lax.rem(me + k, slabs)).wait_send()

    for k in range(1, groups):
        to = lax.rem(group + k, groups)
        pltpu.make_async_remote_copy(
            src_ref=shared.at[group],
            dst_ref=shared.at[group],
            send_sem=sendp_sem.at[to],
            recv_sem=recvp_sem.at[group],
            device_id=(me, to),
            device_id_type=MESH,
        ).wait_send()


def solution(mesh):
    slabs, groups = mesh.shape["slab"], mesh.shape["obs"]

    def local(
        background_members,
        measurement_jitter,
        measurement_readings,
        measurement_noise_spread,
        measurement_grid_location,
        active_tallies,
        coupling_listing,
        taper_factors,
    ):
        own, points = background_members.shape
        span = points // slabs
        cols = span // LANES
        rows = own * cols
        members = own * slabs
        slots = measurement_grid_location.shape[1]
        chunks = slots // LANES
        vmem = pl.BlockSpec(memory_space=pltpu.VMEM)
        smem = pl.BlockSpec(memory_space=pltpu.SMEM)
        f32, bf16 = jnp.float32, jnp.bfloat16
        return pl.pallas_call(
            functools.partial(kernel, slabs, groups),
            out_shape=jax.ShapeDtypeStruct((own, points), f32),
            in_specs=[vmem] * 5 + [smem] * 3,
            out_specs=vmem,
            scratch_shapes=[
                pltpu.VMEM((slabs * rows, LANES), f32),
                pltpu.VMEM((slabs, rows, LANES), bf16),
                pltpu.VMEM((slabs, rows, LANES), bf16),
                pltpu.VMEM((slabs * rows, LANES), f32),
                pltpu.VMEM((cols, members, LANES), f32),
                pltpu.VMEM((cols, members, LANES), bf16),
                pltpu.VMEM((groups, chunks, members // 2, LANES), bf16),
                pltpu.VMEM((groups * chunks, members // 2, LANES), f32),
                pltpu.VMEM((slabs * rows, LANES), f32),
                pltpu.VMEM((slabs, rows, LANES), bf16),
                pltpu.VMEM((slabs, rows, LANES), bf16),
                pltpu.SemaphoreType.DMA((slabs,)),
                pltpu.SemaphoreType.DMA((slabs,)),
                pltpu.SemaphoreType.DMA((groups,)),
                pltpu.SemaphoreType.DMA((groups,)),
                pltpu.SemaphoreType.DMA((slabs,)),
                pltpu.SemaphoreType.DMA((slabs,)),
            ],
            compiler_params=pltpu.CompilerParams(
                collective_id=0, has_side_effects=True, vmem_limit_bytes=48 * 1024 * 1024
            ),
            cost_estimate=pl.CostEstimate(
                flops=200_000_000, bytes_accessed=2_000_000, transcendentals=0
            ),
        )(
            background_members,
            measurement_jitter[:, 0, :],
            measurement_readings,
            measurement_noise_spread,
            measurement_grid_location,
            active_tallies,
            coupling_listing[0].T,
            taper_factors[0].T,
        )

    return jax.shard_map(
        local,
        mesh=mesh,
        in_specs=(
            P("slab", "obs"),
            P(None, "obs", "slab"),
            P("obs", "slab"),
            P("obs", "slab"),
            P("obs", "slab"),
            P("obs", "slab"),
            P("obs", "slab", None),
            P("obs", "slab", None),
        ),
        out_specs=P("slab", "obs"),
        check_vma=False,
    )
```

```python
import functools

import jax
import jax.numpy as jnp
from jax import lax
from jax.experimental import pallas as pl
from jax.experimental.pallas import tpu as pltpu
from jax.sharding import PartitionSpec as P

LANES = 128
MESH = pl.DeviceIdType.MESH


def kernel(
    slabs,
    groups,
    parts,
    bg_hbm,
    jitter_hbm,
    readings_hbm,
    noise_hbm,
    location_hbm,
    tally,
    coupling_hbm,
    taper_hbm,
    out_hbm,
    out,
    bg,
    jitter,
    readings,
    noise,
    location,
    coupling,
    taper,
    rows_f32,
    send1,
    recv1,
    mem_f32,
    tiles,
    prior_all,
    dev,
    shared,
    prod,
    inc_f32,
    send2,
    recv2,
    bg_sem,
    load_sem,
    send1_sem,
    recv1_sem,
    sendp_sem,
    recvp_sem,
    send2_sem,
    recv2_sem,
    out_sem,
):
    own = bg.shape[0]
    span = bg.shape[1] // slabs
    cols = span // LANES
    rows = own * cols
    members = own * slabs
    half = members // 2
    chunks = location.shape[1] // LANES
    links, blocks = coupling.shape
    bundles = members // 8
    per = slabs // bundles
    part_cols = cols // parts
    part_rows = own * part_cols
    me = lax.axis_index("slab")
    group = lax.axis_index("obs")
    home = me // per

    barrier = pltpu.get_barrier_semaphore()

    def bg_load(v):
        at = pl.ds(pl.multiple_of(v * per * span, LANES), per * span)
        return pltpu.make_async_copy(bg_hbm.at[:, at], bg.at[:, at], bg_sem.at[v])

    @pl.loop(0, bundles)
    def _(v):
        bg_load(v).start()

    loads = [
        pltpu.make_async_copy(source, target, load_sem.at[i])
        for i, (source, target) in enumerate(
            (
                (location_hbm, location),
                (jitter_hbm, jitter),
                (readings_hbm, readings),
                (noise_hbm, noise),
                (coupling_hbm, coupling),
                (taper_hbm, taper),
            )
        )
    ]
    for load in loads:
        load.start()

    @pl.loop(1, slabs)
    def _(k):
        pl.semaphore_signal(
            barrier, inc=1, device_id=(lax.rem(me + k, slabs), group), device_id_type=MESH
        )

    for k in range(1, groups):
        pl.semaphore_signal(
            barrier, inc=1, device_id=(me, lax.rem(group + k, groups)), device_id_type=MESH
        )

    @pl.loop(0, bundles)
    def _(v):
        bg_load(v).wait()
        for j in range(per):
            s = v * per + j
            for q in range(cols):
                part = bg[:, pl.ds(pl.multiple_of(s * span + q * LANES, LANES), LANES)]
                if own == 1:
                    rows_f32[pl.ds(s * rows + q, 1), :] = part
                else:
                    rows_f32[pl.ds(s * rows + q, own, stride=cols), :] = part
            send1[s] = rows_f32[pl.ds(pl.multiple_of(s * rows, 16), rows), :].astype(jnp.bfloat16)

    pl.semaphore_wait(barrier, slabs - 1 + groups - 1)

    def forward(to):
        return pltpu.make_async_remote_copy(
            src_ref=send1.at[to],
            dst_ref=recv1.at[me],
            send_sem=send1_sem.at[to],
            recv_sem=recv1_sem.at[me],
            device_id=(to, group),
            device_id_type=MESH,
        )

    def arriving(source):
        return pltpu.make_async_remote_copy(
            src_ref=send1.at[source],
            dst_ref=recv1.at[source],
            send_sem=send1_sem.at[source],
            recv_sem=recv1_sem.at[source],
            device_id=(source, group),
            device_id_type=MESH,
        )

    @pl.loop(1, slabs)
    def _(k):
        forward(lax.rem(me + slabs - k, slabs)).start()

    recv1[me] = send1[me]

    loads[0].wait()
    place = location[...]
    column = [
        jnp.broadcast_to(place[:, c * LANES : (c + 1) * LANES] >> 7, (8, LANES))
        for c in range(chunks)
    ]
    lane = [
        jnp.broadcast_to(place[:, c * LANES : (c + 1) * LANES] & (LANES - 1), (8, LANES))
        for c in range(chunks)
    ]

    @pl.loop(0, bundles)
    def _(k):
        v = lax.rem(home + k, bundles)
        for j in range(per):
            source = v * per + j

            @pl.when(source != me)
            def _():
                arriving(source).wait_recv()

            mem_f32[pl.ds(pl.multiple_of(source * rows, 16), rows), :] = recv1[source].astype(
                jnp.float32
            )
        eight = pl.ds(pl.multiple_of(v * 8, 8), 8)
        values = [jnp.zeros((8, LANES), jnp.float32)] * chunks
        for q in range(cols):
            tile = mem_f32[pl.ds(v * 8 * cols + q, 8, stride=cols), :]
            tiles[q, eight, :] = tile
            for c in range(chunks):
                picked = jnp.take_along_axis(tile, lane[c], axis=1, mode="promise_in_bounds")
                values[c] = jnp.where(column[c] == q, picked, values[c])
        for c in range(chunks):
            prior_all[c, eight, :] = values[c]

    def share(c, to, owner):
        return pltpu.make_async_remote_copy(
            src_ref=shared.at[owner, c],
            dst_ref=shared.at[owner, c],
            send_sem=sendp_sem.at[to, c],
            recv_sem=recvp_sem.at[owner, c],
            device_id=(me, to),
            device_id_type=MESH,
        )

    for load in loads[1:]:
        load.wait()
    live = tally[0, 0]
    lanes = lax.broadcasted_iota(jnp.int32, (members, LANES), 1)
    for c in range(chunks):
        here = slice(c * LANES, (c + 1) * LANES)
        prior = prior_all[c]
        shift = prior - jnp.mean(prior, axis=0, keepdims=True)
        spread = jnp.sum(shift * shift, axis=0, keepdims=True) * (1.0 / (members - 1))
        innovation = (readings[:, here] + jitter[:, here].astype(jnp.float32) - prior) * (
            1.0 / (spread + noise[:, here])
        )
        gain = jnp.where(lanes + c * LANES < live, innovation, 0.0).astype(jnp.bfloat16)
        product = lax.dot_general(
            gain,
            shift.astype(jnp.bfloat16),
            (((1,), (1,)), ((), ())),
            preferred_element_type=jnp.float32,
        )
        packed = jnp.concatenate([product[:half], product[half:]], axis=1)
        prod[group * chunks + c] = packed
        shared[group, c] = packed.astype(jnp.bfloat16)
        for k in range(1, groups):
            share(c, lax.rem(group + k, groups), group).start()

    for q in range(cols):
        tile = tiles[q]
        dev[q] = (tile - jnp.mean(tile, axis=0, keepdims=True)).astype(jnp.bfloat16)

    for k in range(1, groups):
        source = lax.rem(group + k, groups)
        for c in range(chunks):
            share(c, source, source).wait_recv()
            prod[source * chunks + c] = shared[source, c].astype(jnp.float32)

    low_lane = lax.broadcasted_iota(jnp.int32, (2 * half, LANES), 1) < LANES // 2
    low_half = lax.broadcasted_iota(jnp.int32, (half, LANES), 1) < LANES // 2

    def backward(h, to):
        return pltpu.make_async_remote_copy(
            src_ref=send2.at[h, to],
            dst_ref=recv2.at[h, me],
            send_sem=send2_sem.at[h, to],
            recv_sem=recv2_sem.at[h, me],
            device_id=(to, group),
            device_id_type=MESH,
        )

    def back(h, source):
        return pltpu.make_async_remote_copy(
            src_ref=send2.at[h, source],
            dst_ref=recv2.at[h, source],
            send_sem=send2_sem.at[h, source],
            recv_sem=recv2_sem.at[h, source],
            device_id=(source, group),
            device_id_type=MESH,
        )

    for h in range(parts):
        for i in range(part_cols):
            q = h * part_cols + i
            pair = []
            for b in (2 * q, 2 * q + 1):
                total = taper[0, b] * prod[coupling[0, b]]
                for l in range(1, links):
                    total = total + taper[l, b] * prod[coupling[l, b]]
                pair.append(total * (1.0 / (members - 1)))
            pair = jnp.concatenate(pair, axis=0)
            left = jnp.concatenate(
                [jnp.where(low_lane, pair, 0.0), jnp.where(low_lane, 0.0, pair)], axis=0
            ).astype(jnp.bfloat16)
            right = dev[q]
            right = jnp.concatenate([right, right], axis=0)
            update = jnp.dot(left, right, preferred_element_type=jnp.float32)
            inc_f32[h, pl.ds(i, half, stride=part_cols), :] = jnp.where(
                low_half, update[:half], update[half : 2 * half]
            )
            inc_f32[h, pl.ds(i + half * part_cols, half, stride=part_cols), :] = jnp.where(
                low_half, update[2 * half : 3 * half], update[3 * half :]
            )

        @pl.loop(1, slabs)
        def _(k):
            to = lax.rem(me + slabs - k, slabs)
            send2[h, to] = inc_f32[
                h, pl.ds(pl.multiple_of(to * part_rows, 16), part_rows), :
            ].astype(jnp.bfloat16)
            backward(h, to).start()

    def finish(h, s, low):
        base = s * rows + h * part_rows
        rows_f32[pl.ds(pl.multiple_of(base, 16), part_rows), :] = low.astype(jnp.float32)
        for i in range(part_cols):
            q = h * part_cols + i
            at = pl.ds(pl.multiple_of(s * span + q * LANES, LANES), LANES)
            if own == 1:
                part = rows_f32[pl.ds(base + i, 1), :]
            else:
                part = rows_f32[pl.ds(base + i, own, stride=part_cols), :]
            out[:, at] = bg[:, at] + part

    def out_copy(s):
        at = pl.ds(pl.multiple_of(s * span, LANES), span)
        return pltpu.make_async_copy(out.at[:, at], out_hbm.at[:, at], out_sem.at[s])

    for h in range(parts):
        finish(
            h,
            me,
            inc_f32[h, pl.ds(pl.multiple_of(me * part_rows, 16), part_rows), :].astype(
                jnp.bfloat16
            ),
        )
        if h == parts - 1:
            out_copy(me).start()

        @pl.loop(1, slabs)
        def _(k):
            source = lax.rem(me + k, slabs)
            back(h, source).wait_recv()
            finish(h, source, recv2[h, source])
            if h == parts - 1:
                out_copy(source).start()

    @pl.loop(1, slabs)
    def _(k):
        to = lax.rem(me + k, slabs)
        forward(to).wait_send()
        for h in range(parts):
            backward(h, to).wait_send()
        out_copy(to).wait()

    out_copy(me).wait()

    for k in range(1, groups):
        to = lax.rem(group + k, groups)
        for c in range(chunks):
            share(c, to, group).wait_send()


def solution(mesh):
    slabs, groups = mesh.shape["slab"], mesh.shape["obs"]

    def local(
        background_members,
        measurement_jitter,
        measurement_readings,
        measurement_noise_spread,
        measurement_grid_location,
        active_tallies,
        coupling_listing,
        taper_factors,
    ):
        own, points = background_members.shape
        span = points // slabs
        cols = span // LANES
        rows = own * cols
        members = own * slabs
        slots = measurement_grid_location.shape[1]
        chunks = slots // LANES
        blocks, links = coupling_listing.shape[1:]
        parts = 2 if rows % 32 == 0 else 1
        smem = pl.BlockSpec(memory_space=pltpu.SMEM)
        hbm = pl.BlockSpec(memory_space=pl.ANY)
        f32, bf16, i32 = jnp.float32, jnp.bfloat16, jnp.int32
        return pl.pallas_call(
            functools.partial(kernel, slabs, groups, parts),
            out_shape=jax.ShapeDtypeStruct((own, points), f32),
            in_specs=[hbm] * 5 + [smem] + [hbm] * 2,
            out_specs=hbm,
            scratch_shapes=[
                pltpu.VMEM((own, points), f32),
                pltpu.VMEM((own, points), f32),
                pltpu.VMEM((members, slots), bf16),
                pltpu.VMEM((1, slots), f32),
                pltpu.VMEM((1, slots), f32),
                pltpu.VMEM((1, slots), i32),
                pltpu.SMEM((links, blocks), i32),
                pltpu.SMEM((links, blocks), f32),
                pltpu.VMEM((slabs * rows, LANES), f32),
                pltpu.VMEM((slabs, rows, LANES), bf16),
                pltpu.VMEM((slabs, rows, LANES), bf16),
                pltpu.VMEM((slabs * rows, LANES), f32),
                pltpu.VMEM((cols, members, LANES), f32),
                pltpu.VMEM((chunks, members, LANES), f32),
                pltpu.VMEM((cols, members, LANES), bf16),
                pltpu.VMEM((groups, chunks, members // 2, LANES), bf16),
                pltpu.VMEM((groups * chunks, members // 2, LANES), f32),
                pltpu.VMEM((parts, slabs * rows // parts, LANES), f32),
                pltpu.VMEM((parts, slabs, rows // parts, LANES), bf16),
                pltpu.VMEM((parts, slabs, rows // parts, LANES), bf16),
                pltpu.SemaphoreType.DMA((members // 8,)),
                pltpu.SemaphoreType.DMA((6,)),
                pltpu.SemaphoreType.DMA((slabs,)),
                pltpu.SemaphoreType.DMA((slabs,)),
                pltpu.SemaphoreType.DMA((groups, chunks)),
                pltpu.SemaphoreType.DMA((groups, chunks)),
                pltpu.SemaphoreType.DMA((parts, slabs)),
                pltpu.SemaphoreType.DMA((parts, slabs)),
                pltpu.SemaphoreType.DMA((slabs,)),
            ],
            compiler_params=pltpu.CompilerParams(
                collective_id=0, has_side_effects=True, vmem_limit_bytes=60 * 1024 * 1024
            ),
            cost_estimate=pl.CostEstimate(
                flops=200_000_000, bytes_accessed=2_000_000, transcendentals=0
            ),
        )(
            background_members,
            measurement_jitter[:, 0, :],
            measurement_readings,
            measurement_noise_spread,
            measurement_grid_location,
            active_tallies,
            coupling_listing[0].T,
            taper_factors[0].T,
        )

    return jax.shard_map(
        local,
        mesh=mesh,
        in_specs=(
            P("slab", "obs"),
            P(None, "obs", "slab"),
            P("obs", "slab"),
            P("obs", "slab"),
            P("obs", "slab"),
            P("obs", "slab"),
            P("obs", "slab", None),
            P("obs", "slab", None),
        ),
        out_specs=P("slab", "obs"),
        check_vma=False,
    )
```

```python
import functools

import jax
import jax.numpy as jnp
from jax import lax
from jax.experimental import pallas as pl
from jax.experimental.pallas import tpu as pltpu
from jax.sharding import PartitionSpec as P

LANES = 128
MESH = pl.DeviceIdType.MESH


def kernel(
    slabs,
    groups,
    parts,
    bg_hbm,
    jitter_hbm,
    readings_hbm,
    noise_hbm,
    location_hbm,
    tally,
    coupling_hbm,
    taper_hbm,
    out,
    bg,
    jitter,
    readings,
    noise,
    location,
    coupling,
    taper,
    rows_f32,
    send1,
    recv1,
    mem_f32,
    tiles,
    prior_all,
    dev,
    shared,
    prod,
    inc_f32,
    send2,
    recv2,
    bg_sem,
    load_sem,
    send1_sem,
    recv1_sem,
    sendp_sem,
    recvp_sem,
    send2_sem,
    recv2_sem,
):
    own = bg.shape[0]
    span = bg.shape[1] // slabs
    cols = span // LANES
    rows = own * cols
    members = own * slabs
    half = members // 2
    chunks = location.shape[1] // LANES
    links, blocks = coupling.shape
    bundles = members // 8
    per = slabs // bundles
    part_cols = cols // parts
    part_rows = own * part_cols
    me = lax.axis_index("slab")
    group = lax.axis_index("obs")
    home = me // per

    barrier = pltpu.get_barrier_semaphore()

    @pl.loop(1, slabs)
    def _(k):
        pl.semaphore_signal(
            barrier, inc=1, device_id=(lax.rem(me + k, slabs), group), device_id_type=MESH
        )

    for k in range(1, groups):
        pl.semaphore_signal(
            barrier, inc=1, device_id=(me, lax.rem(group + k, groups)), device_id_type=MESH
        )

    def bg_load(v):
        at = pl.ds(pl.multiple_of(v * per * span, LANES), per * span)
        return pltpu.make_async_copy(bg_hbm.at[:, at], bg.at[:, at], bg_sem.at[v])

    @pl.loop(0, bundles)
    def _(k):
        bg_load(lax.rem(home + 2 * bundles - 1 - k, bundles)).start()

    loads = [
        pltpu.make_async_copy(source, target, load_sem.at[i])
        for i, (source, target) in enumerate(
            (
                (location_hbm, location),
                (jitter_hbm, jitter),
                (readings_hbm, readings),
                (noise_hbm, noise),
                (coupling_hbm, coupling),
                (taper_hbm, taper),
            )
        )
    ]
    for load in loads:
        load.start()

    def forward(to):
        return pltpu.make_async_remote_copy(
            src_ref=send1.at[to],
            dst_ref=recv1.at[me],
            send_sem=send1_sem.at[to],
            recv_sem=recv1_sem.at[me],
            device_id=(to, group),
            device_id_type=MESH,
        )

    def arriving(source):
        return pltpu.make_async_remote_copy(
            src_ref=send1.at[source],
            dst_ref=recv1.at[source],
            send_sem=send1_sem.at[source],
            recv_sem=recv1_sem.at[source],
            device_id=(source, group),
            device_id_type=MESH,
        )

    def pack(k):
        v = lax.rem(home + 2 * bundles - 1 - k, bundles)
        bg_load(v).wait()
        for j in range(per):
            s = v * per + j
            for q in range(cols):
                part = bg[:, pl.ds(pl.multiple_of(s * span + q * LANES, LANES), LANES)]
                if own == 1:
                    rows_f32[pl.ds(s * rows + q, 1), :] = part
                else:
                    rows_f32[pl.ds(s * rows + q, own, stride=cols), :] = part
            send1[s] = rows_f32[pl.ds(pl.multiple_of(s * rows, 16), rows), :].astype(jnp.bfloat16)

    def send(k):
        v = lax.rem(home + 2 * bundles - 1 - k, bundles)
        for j in range(per):
            to = v * per + j

            @pl.when(to != me)
            def _():
                forward(to).start()

    early = 2

    @pl.loop(0, early)
    def _(k):
        pack(k)

    pl.semaphore_wait(barrier, slabs - 1 + groups - 1)

    @pl.loop(0, early)
    def _(k):
        send(k)

    @pl.loop(early, bundles)
    def _(k):
        pack(k)
        send(k)

    recv1[me] = send1[me]

    loads[0].wait()
    place = location[...]
    column = [
        jnp.broadcast_to(place[:, c * LANES : (c + 1) * LANES] >> 7, (8, LANES))
        for c in range(chunks)
    ]
    lane = [
        jnp.broadcast_to(place[:, c * LANES : (c + 1) * LANES] & (LANES - 1), (8, LANES))
        for c in range(chunks)
    ]

    @pl.loop(0, bundles)
    def _(k):
        v = lax.rem(home + 1 + k, bundles)
        for j in range(per):
            source = v * per + j

            @pl.when(source != me)
            def _():
                arriving(source).wait_recv()

            mem_f32[pl.ds(pl.multiple_of(source * rows, 16), rows), :] = recv1[source].astype(
                jnp.float32
            )
        eight = pl.ds(pl.multiple_of(v * 8, 8), 8)
        values = [jnp.zeros((8, LANES), jnp.float32)] * chunks
        for q in range(cols):
            tile = mem_f32[pl.ds(v * 8 * cols + q, 8, stride=cols), :]
            tiles[q, eight, :] = tile
            for c in range(chunks):
                picked = jnp.take_along_axis(tile, lane[c], axis=1, mode="promise_in_bounds")
                values[c] = jnp.where(column[c] == q, picked, values[c])
        for c in range(chunks):
            prior_all[c, eight, :] = values[c]

    def share(c, to, owner):
        return pltpu.make_async_remote_copy(
            src_ref=shared.at[owner, c],
            dst_ref=shared.at[owner, c],
            send_sem=sendp_sem.at[to, c],
            recv_sem=recvp_sem.at[owner, c],
            device_id=(me, to),
            device_id_type=MESH,
        )

    for load in loads[1:]:
        load.wait()
    live = tally[0, 0]
    lanes = lax.broadcasted_iota(jnp.int32, (members, LANES), 1)
    for c in range(chunks):
        here = slice(c * LANES, (c + 1) * LANES)
        prior = prior_all[c]
        shift = prior - jnp.mean(prior, axis=0, keepdims=True)
        spread = jnp.sum(shift * shift, axis=0, keepdims=True) * (1.0 / (members - 1))
        innovation = (readings[:, here] + jitter[:, here].astype(jnp.float32) - prior) * (
            1.0 / (spread + noise[:, here])
        )
        gain = jnp.where(lanes + c * LANES < live, innovation, 0.0).astype(jnp.bfloat16)
        product = lax.dot_general(
            gain,
            shift.astype(jnp.bfloat16),
            (((1,), (1,)), ((), ())),
            preferred_element_type=jnp.float32,
        )
        packed = jnp.concatenate([product[:half], product[half:]], axis=1)
        prod[group * chunks + c] = packed
        shared[group, c] = packed.astype(jnp.bfloat16)
        for k in range(1, groups):
            share(c, lax.rem(group + k, groups), group).start()

    for q in range(cols):
        tile = tiles[q]
        dev[q] = (tile - jnp.mean(tile, axis=0, keepdims=True)).astype(jnp.bfloat16)

    for k in range(1, groups):
        source = lax.rem(group + k, groups)
        for c in range(chunks):
            share(c, source, source).wait_recv()
            prod[source * chunks + c] = shared[source, c].astype(jnp.float32)

    low_lane = lax.broadcasted_iota(jnp.int32, (2 * half, LANES), 1) < LANES // 2
    low_half = lax.broadcasted_iota(jnp.int32, (half, LANES), 1) < LANES // 2

    def backward(h, to):
        return pltpu.make_async_remote_copy(
            src_ref=send2.at[h, to],
            dst_ref=recv2.at[h, me],
            send_sem=send2_sem.at[h, to],
            recv_sem=recv2_sem.at[h, me],
            device_id=(to, group),
            device_id_type=MESH,
        )

    def back(h, source):
        return pltpu.make_async_remote_copy(
            src_ref=send2.at[h, source],
            dst_ref=recv2.at[h, source],
            send_sem=send2_sem.at[h, source],
            recv_sem=recv2_sem.at[h, source],
            device_id=(source, group),
            device_id_type=MESH,
        )

    for h in range(parts):
        for i in range(part_cols):
            q = h * part_cols + i
            pair = []
            for b in (2 * q, 2 * q + 1):
                total = taper[0, b] * prod[coupling[0, b]]
                for l in range(1, links):
                    total = total + taper[l, b] * prod[coupling[l, b]]
                pair.append(total * (1.0 / (members - 1)))
            pair = jnp.concatenate(pair, axis=0)
            left = jnp.concatenate(
                [jnp.where(low_lane, pair, 0.0), jnp.where(low_lane, 0.0, pair)], axis=0
            ).astype(jnp.bfloat16)
            right = dev[q]
            right = jnp.concatenate([right, right], axis=0)
            update = jnp.dot(left, right, preferred_element_type=jnp.float32)
            inc_f32[h, pl.ds(i, half, stride=part_cols), :] = jnp.where(
                low_half, update[:half], update[half : 2 * half]
            )
            inc_f32[h, pl.ds(i + half * part_cols, half, stride=part_cols), :] = jnp.where(
                low_half, update[2 * half : 3 * half], update[3 * half :]
            )

        @pl.loop(1, slabs)
        def _(k):
            to = lax.rem(me + slabs - k, slabs)
            send2[h, to] = inc_f32[
                h, pl.ds(pl.multiple_of(to * part_rows, 16), part_rows), :
            ].astype(jnp.bfloat16)
            backward(h, to).start()

    def finish(h, s, low):
        base = s * rows + h * part_rows
        rows_f32[pl.ds(pl.multiple_of(base, 16), part_rows), :] = low.astype(jnp.float32)
        for i in range(part_cols):
            q = h * part_cols + i
            at = pl.ds(pl.multiple_of(s * span + q * LANES, LANES), LANES)
            if own == 1:
                part = rows_f32[pl.ds(base + i, 1), :]
            else:
                part = rows_f32[pl.ds(base + i, own, stride=part_cols), :]
            out[:, at] = bg[:, at] + part

    for h in range(parts):
        finish(
            h,
            me,
            inc_f32[h, pl.ds(pl.multiple_of(me * part_rows, 16), part_rows), :].astype(
                jnp.bfloat16
            ),
        )

        @pl.loop(1, slabs)
        def _(k):
            source = lax.rem(me + k, slabs)
            back(h, source).wait_recv()
            finish(h, source, recv2[h, source])

    @pl.loop(1, slabs)
    def _(k):
        to = lax.rem(me + k, slabs)
        forward(to).wait_send()
        for h in range(parts):
            backward(h, to).wait_send()

    for k in range(1, groups):
        to = lax.rem(group + k, groups)
        for c in range(chunks):
            share(c, to, group).wait_send()


def solution(mesh):
    slabs, groups = mesh.shape["slab"], mesh.shape["obs"]

    def local(
        background_members,
        measurement_jitter,
        measurement_readings,
        measurement_noise_spread,
        measurement_grid_location,
        active_tallies,
        coupling_listing,
        taper_factors,
    ):
        own, points = background_members.shape
        span = points // slabs
        cols = span // LANES
        rows = own * cols
        members = own * slabs
        slots = measurement_grid_location.shape[1]
        chunks = slots // LANES
        blocks, links = coupling_listing.shape[1:]
        parts = 2 if rows % 32 == 0 else 1
        smem = pl.BlockSpec(memory_space=pltpu.SMEM)
        hbm = pl.BlockSpec(memory_space=pl.ANY)
        f32, bf16, i32 = jnp.float32, jnp.bfloat16, jnp.int32
        return pl.pallas_call(
            functools.partial(kernel, slabs, groups, parts),
            out_shape=pltpu.VMEM((own, points), f32),
            in_specs=[hbm] * 5 + [smem] + [hbm] * 2,
            out_specs=pl.BlockSpec(memory_space=pltpu.VMEM),
            scratch_shapes=[
                pltpu.VMEM((own, points), f32),
                pltpu.VMEM((members, slots), bf16),
                pltpu.VMEM((1, slots), f32),
                pltpu.VMEM((1, slots), f32),
                pltpu.VMEM((1, slots), i32),
                pltpu.SMEM((links, blocks), i32),
                pltpu.SMEM((links, blocks), f32),
                pltpu.VMEM((slabs * rows, LANES), f32),
                pltpu.VMEM((slabs, rows, LANES), bf16),
                pltpu.VMEM((slabs, rows, LANES), bf16),
                pltpu.VMEM((slabs * rows, LANES), f32),
                pltpu.VMEM((cols, members, LANES), f32),
                pltpu.VMEM((chunks, members, LANES), f32),
                pltpu.VMEM((cols, members, LANES), bf16),
                pltpu.VMEM((groups, chunks, members // 2, LANES), bf16),
                pltpu.VMEM((groups * chunks, members // 2, LANES), f32),
                pltpu.VMEM((parts, slabs * rows // parts, LANES), f32),
                pltpu.VMEM((parts, slabs, rows // parts, LANES), bf16),
                pltpu.VMEM((parts, slabs, rows // parts, LANES), bf16),
                pltpu.SemaphoreType.DMA((members // 8,)),
                pltpu.SemaphoreType.DMA((6,)),
                pltpu.SemaphoreType.DMA((slabs,)),
                pltpu.SemaphoreType.DMA((slabs,)),
                pltpu.SemaphoreType.DMA((groups, chunks)),
                pltpu.SemaphoreType.DMA((groups, chunks)),
                pltpu.SemaphoreType.DMA((parts, slabs)),
                pltpu.SemaphoreType.DMA((parts, slabs)),
            ],
            compiler_params=pltpu.CompilerParams(
                collective_id=0, has_side_effects=True, vmem_limit_bytes=60 * 1024 * 1024
            ),
            cost_estimate=pl.CostEstimate(
                flops=200_000_000, bytes_accessed=2_000_000, transcendentals=0
            ),
        )(
            background_members,
            measurement_jitter[:, 0, :],
            measurement_readings,
            measurement_noise_spread,
            measurement_grid_location,
            active_tallies,
            coupling_listing[0].T,
            taper_factors[0].T,
        )

    return jax.shard_map(
        local,
        mesh=mesh,
        in_specs=(
            P("slab", "obs"),
            P(None, "obs", "slab"),
            P("obs", "slab"),
            P("obs", "slab"),
            P("obs", "slab"),
            P("obs", "slab"),
            P("obs", "slab", None),
            P("obs", "slab", None),
        ),
        out_specs=P("slab", "obs"),
        check_vma=False,
    )
```

```python
import functools

import jax
import jax.numpy as jnp
from jax import lax
from jax.experimental import pallas as pl
from jax.experimental.pallas import tpu as pltpu
from jax.sharding import PartitionSpec as P

LANES = 128
MESH = pl.DeviceIdType.MESH


def kernel(
    slabs,
    groups,
    parts,
    bg_hbm,
    jitter_hbm,
    readings_hbm,
    noise_hbm,
    location_hbm,
    tally,
    coupling_hbm,
    taper_hbm,
    out,
    bg,
    jitter,
    readings,
    noise,
    location,
    coupling,
    taper,
    rows_f32,
    send1,
    recv1,
    mem_f32,
    tiles,
    prior_all,
    dev,
    shared,
    prod,
    inc_f32,
    send2,
    recv2,
    bg_sem,
    load_sem,
    send1_sem,
    recv1_sem,
    sendp_sem,
    recvp_sem,
    send2_sem,
    recv2_sem,
):
    own = bg.shape[0]
    span = bg.shape[1] // slabs
    cols = span // LANES
    rows = own * cols
    members = own * slabs
    half = members // 2
    chunks = location.shape[1] // LANES
    links, blocks = coupling.shape
    bundles = members // 8
    per = slabs // bundles
    part_cols = cols // parts
    part_rows = own * part_cols
    me = lax.axis_index("slab")
    group = lax.axis_index("obs")
    home = me // per
    depth = bundles // 2

    def ahead(k):
        j = lax.rem(k + 2, bundles)
        z = lax.rem(home // 2 + depth - j // 2, depth)
        return z * 2 + lax.rem(home + j, 2)

    def behind(k):
        j = lax.rem(k + 2, bundles)
        z = lax.rem(home // 2 + j // 2, depth)
        return z * 2 + lax.rem(home + j, 2)

    barrier = pltpu.get_barrier_semaphore()

    @pl.loop(1, slabs)
    def _(k):
        pl.semaphore_signal(
            barrier, inc=1, device_id=(lax.rem(me + k, slabs), group), device_id_type=MESH
        )

    for k in range(1, groups):
        pl.semaphore_signal(
            barrier, inc=1, device_id=(me, lax.rem(group + k, groups)), device_id_type=MESH
        )

    def bg_load(v):
        at = pl.ds(pl.multiple_of(v * per * span, LANES), per * span)
        return pltpu.make_async_copy(bg_hbm.at[:, at], bg.at[:, at], bg_sem.at[v])

    @pl.loop(0, bundles)
    def _(k):
        bg_load(ahead(k)).start()

    loads = [
        pltpu.make_async_copy(source, target, load_sem.at[i])
        for i, (source, target) in enumerate(
            (
                (location_hbm, location),
                (jitter_hbm, jitter),
                (readings_hbm, readings),
                (noise_hbm, noise),
                (coupling_hbm, coupling),
                (taper_hbm, taper),
            )
        )
    ]
    for load in loads:
        load.start()

    def forward(to):
        return pltpu.make_async_remote_copy(
            src_ref=send1.at[to],
            dst_ref=recv1.at[me],
            send_sem=send1_sem.at[to],
            recv_sem=recv1_sem.at[me],
            device_id=(to, group),
            device_id_type=MESH,
        )

    def arriving(source):
        return pltpu.make_async_remote_copy(
            src_ref=send1.at[source],
            dst_ref=recv1.at[source],
            send_sem=send1_sem.at[source],
            recv_sem=recv1_sem.at[source],
            device_id=(source, group),
            device_id_type=MESH,
        )

    def pack(k):
        v = ahead(k)
        bg_load(v).wait()
        for j in range(per):
            s = v * per + j
            for q in range(cols):
                part = bg[:, pl.ds(pl.multiple_of(s * span + q * LANES, LANES), LANES)]
                if own == 1:
                    rows_f32[pl.ds(s * rows + q, 1), :] = part
                else:
                    rows_f32[pl.ds(s * rows + q, own, stride=cols), :] = part
            send1[s] = rows_f32[pl.ds(pl.multiple_of(s * rows, 16), rows), :].astype(jnp.bfloat16)

    def send(k):
        v = ahead(k)
        for j in range(per):
            to = v * per + j

            @pl.when(to != me)
            def _():
                forward(to).start()

    @pl.loop(0, bundles)
    def _(k):
        pack(k)

    pl.semaphore_wait(barrier, slabs - 1 + groups - 1)

    @pl.loop(0, bundles)
    def _(k):
        send(k)

    recv1[me] = send1[me]

    loads[0].wait()
    place = location[...]
    column = [
        jnp.broadcast_to(place[:, c * LANES : (c + 1) * LANES] >> 7, (8, LANES))
        for c in range(chunks)
    ]
    lane = [
        jnp.broadcast_to(place[:, c * LANES : (c + 1) * LANES] & (LANES - 1), (8, LANES))
        for c in range(chunks)
    ]

    @pl.loop(0, bundles)
    def _(k):
        v = behind(k)
        for j in range(per):
            source = v * per + j

            @pl.when(source != me)
            def _():
                arriving(source).wait_recv()

            mem_f32[pl.ds(pl.multiple_of(source * rows, 16), rows), :] = recv1[source].astype(
                jnp.float32
            )
        eight = pl.ds(pl.multiple_of(v * 8, 8), 8)
        values = [jnp.zeros((8, LANES), jnp.float32)] * chunks
        for q in range(cols):
            tile = mem_f32[pl.ds(v * 8 * cols + q, 8, stride=cols), :]
            tiles[q, eight, :] = tile
            for c in range(chunks):
                picked = jnp.take_along_axis(tile, lane[c], axis=1, mode="promise_in_bounds")
                values[c] = jnp.where(column[c] == q, picked, values[c])
        for c in range(chunks):
            prior_all[c, eight, :] = values[c]

    def share(c, to, owner):
        return pltpu.make_async_remote_copy(
            src_ref=shared.at[owner, c],
            dst_ref=shared.at[owner, c],
            send_sem=sendp_sem.at[to, c],
            recv_sem=recvp_sem.at[owner, c],
            device_id=(me, to),
            device_id_type=MESH,
        )

    for load in loads[1:]:
        load.wait()
    live = tally[0, 0]
    lanes = lax.broadcasted_iota(jnp.int32, (members, LANES), 1)
    for c in range(chunks):
        here = slice(c * LANES, (c + 1) * LANES)
        prior = prior_all[c]
        shift = prior - jnp.mean(prior, axis=0, keepdims=True)
        spread = jnp.sum(shift * shift, axis=0, keepdims=True) * (1.0 / (members - 1))
        innovation = (readings[:, here] + jitter[:, here].astype(jnp.float32) - prior) * (
            1.0 / (spread + noise[:, here])
        )
        gain = jnp.where(lanes + c * LANES < live, innovation, 0.0).astype(jnp.bfloat16)
        product = lax.dot_general(
            gain,
            shift.astype(jnp.bfloat16),
            (((1,), (1,)), ((), ())),
            preferred_element_type=jnp.float32,
        )
        packed = jnp.concatenate([product[:half], product[half:]], axis=1)
        prod[group * chunks + c] = packed
        shared[group, c] = packed.astype(jnp.bfloat16)
        for k in range(1, groups):
            share(c, lax.rem(group + k, groups), group).start()

    for q in range(cols):
        tile = tiles[q]
        dev[q] = (tile - jnp.mean(tile, axis=0, keepdims=True)).astype(jnp.bfloat16)

    for k in range(1, groups):
        source = lax.rem(group + k, groups)
        for c in range(chunks):
            share(c, source, source).wait_recv()
            prod[source * chunks + c] = shared[source, c].astype(jnp.float32)

    low_lane = lax.broadcasted_iota(jnp.int32, (2 * half, LANES), 1) < LANES // 2
    low_half = lax.broadcasted_iota(jnp.int32, (half, LANES), 1) < LANES // 2

    def backward(h, to):
        return pltpu.make_async_remote_copy(
            src_ref=send2.at[h, to],
            dst_ref=recv2.at[h, me],
            send_sem=send2_sem.at[h, to],
            recv_sem=recv2_sem.at[h, me],
            device_id=(to, group),
            device_id_type=MESH,
        )

    def back(h, source):
        return pltpu.make_async_remote_copy(
            src_ref=send2.at[h, source],
            dst_ref=recv2.at[h, source],
            send_sem=send2_sem.at[h, source],
            recv_sem=recv2_sem.at[h, source],
            device_id=(source, group),
            device_id_type=MESH,
        )

    for h in range(parts):
        for i in range(part_cols):
            q = h * part_cols + i
            pair = []
            for b in (2 * q, 2 * q + 1):
                total = taper[0, b] * prod[coupling[0, b]]
                for l in range(1, links):
                    total = total + taper[l, b] * prod[coupling[l, b]]
                pair.append(total * (1.0 / (members - 1)))
            pair = jnp.concatenate(pair, axis=0)
            left = jnp.concatenate(
                [jnp.where(low_lane, pair, 0.0), jnp.where(low_lane, 0.0, pair)], axis=0
            ).astype(jnp.bfloat16)
            right = dev[q]
            right = jnp.concatenate([right, right], axis=0)
            update = jnp.dot(left, right, preferred_element_type=jnp.float32)
            inc_f32[h, pl.ds(i, half, stride=part_cols), :] = jnp.where(
                low_half, update[:half], update[half : 2 * half]
            )
            inc_f32[h, pl.ds(i + half * part_cols, half, stride=part_cols), :] = jnp.where(
                low_half, update[2 * half : 3 * half], update[3 * half :]
            )

        @pl.loop(0, bundles)
        def _(k):
            for j in range(per):
                to = ahead(k) * per + j
                send2[h, to] = inc_f32[
                    h, pl.ds(pl.multiple_of(to * part_rows, 16), part_rows), :
                ].astype(jnp.bfloat16)

                @pl.when(to != me)
                def _():
                    backward(h, to).start()

    def finish(h, s, low):
        base = s * rows + h * part_rows
        rows_f32[pl.ds(pl.multiple_of(base, 16), part_rows), :] = low.astype(jnp.float32)
        for i in range(part_cols):
            q = h * part_cols + i
            at = pl.ds(pl.multiple_of(s * span + q * LANES, LANES), LANES)
            if own == 1:
                part = rows_f32[pl.ds(base + i, 1), :]
            else:
                part = rows_f32[pl.ds(base + i, own, stride=part_cols), :]
            out[:, at] = bg[:, at] + part

    for h in range(parts):
        recv2[h, me] = send2[h, me]

        @pl.loop(0, bundles)
        def _(k):
            for j in range(per):
                source = behind(k) * per + j

                @pl.when(source != me)
                def _():
                    back(h, source).wait_recv()

                finish(h, source, recv2[h, source])

    @pl.loop(1, slabs)
    def _(k):
        to = lax.rem(me + k, slabs)
        forward(to).wait_send()
        for h in range(parts):
            backward(h, to).wait_send()

    for k in range(1, groups):
        to = lax.rem(group + k, groups)
        for c in range(chunks):
            share(c, to, group).wait_send()


def solution(mesh):
    slabs, groups = mesh.shape["slab"], mesh.shape["obs"]

    def local(
        background_members,
        measurement_jitter,
        measurement_readings,
        measurement_noise_spread,
        measurement_grid_location,
        active_tallies,
        coupling_listing,
        taper_factors,
    ):
        own, points = background_members.shape
        span = points // slabs
        cols = span // LANES
        rows = own * cols
        members = own * slabs
        slots = measurement_grid_location.shape[1]
        chunks = slots // LANES
        blocks, links = coupling_listing.shape[1:]
        parts = 2 if rows % 32 == 0 else 1
        smem = pl.BlockSpec(memory_space=pltpu.SMEM)
        hbm = pl.BlockSpec(memory_space=pl.ANY)
        f32, bf16, i32 = jnp.float32, jnp.bfloat16, jnp.int32
        return pl.pallas_call(
            functools.partial(kernel, slabs, groups, parts),
            out_shape=pltpu.VMEM((own, points), f32),
            in_specs=[hbm] * 5 + [smem] + [hbm] * 2,
            out_specs=pl.BlockSpec(memory_space=pltpu.VMEM),
            scratch_shapes=[
                pltpu.VMEM((own, points), f32),
                pltpu.VMEM((members, slots), bf16),
                pltpu.VMEM((1, slots), f32),
                pltpu.VMEM((1, slots), f32),
                pltpu.VMEM((1, slots), i32),
                pltpu.SMEM((links, blocks), i32),
                pltpu.SMEM((links, blocks), f32),
                pltpu.VMEM((slabs * rows, LANES), f32),
                pltpu.VMEM((slabs, rows, LANES), bf16),
                pltpu.VMEM((slabs, rows, LANES), bf16),
                pltpu.VMEM((slabs * rows, LANES), f32),
                pltpu.VMEM((cols, members, LANES), f32),
                pltpu.VMEM((chunks, members, LANES), f32),
                pltpu.VMEM((cols, members, LANES), bf16),
                pltpu.VMEM((groups, chunks, members // 2, LANES), bf16),
                pltpu.VMEM((groups * chunks, members // 2, LANES), f32),
                pltpu.VMEM((parts, slabs * rows // parts, LANES), f32),
                pltpu.VMEM((parts, slabs, rows // parts, LANES), bf16),
                pltpu.VMEM((parts, slabs, rows // parts, LANES), bf16),
                pltpu.SemaphoreType.DMA((members // 8,)),
                pltpu.SemaphoreType.DMA((6,)),
                pltpu.SemaphoreType.DMA((slabs,)),
                pltpu.SemaphoreType.DMA((slabs,)),
                pltpu.SemaphoreType.DMA((groups, chunks)),
                pltpu.SemaphoreType.DMA((groups, chunks)),
                pltpu.SemaphoreType.DMA((parts, slabs)),
                pltpu.SemaphoreType.DMA((parts, slabs)),
            ],
            compiler_params=pltpu.CompilerParams(
                collective_id=0, has_side_effects=True, vmem_limit_bytes=60 * 1024 * 1024
            ),
            cost_estimate=pl.CostEstimate(
                flops=200_000_000, bytes_accessed=2_000_000, transcendentals=0
            ),
        )(
            background_members,
            measurement_jitter[:, 0, :],
            measurement_readings,
            measurement_noise_spread,
            measurement_grid_location,
            active_tallies,
            coupling_listing[0].T,
            taper_factors[0].T,
        )

    return jax.shard_map(
        local,
        mesh=mesh,
        in_specs=(
            P("slab", "obs"),
            P(None, "obs", "slab"),
            P("obs", "slab"),
            P("obs", "slab"),
            P("obs", "slab"),
            P("obs", "slab"),
            P("obs", "slab", None),
            P("obs", "slab", None),
        ),
        out_specs=P("slab", "obs"),
        check_vma=False,
    )
```

```python
import functools

import jax
import jax.numpy as jnp
from jax import lax
from jax.experimental import pallas as pl
from jax.experimental.pallas import tpu as pltpu
from jax.sharding import PartitionSpec as P

LANES = 128
MESH = pl.DeviceIdType.MESH


def kernel(
    slabs,
    groups,
    parts,
    bg_hbm,
    jitter_hbm,
    readings_hbm,
    noise_hbm,
    location_hbm,
    tally,
    coupling_hbm,
    taper_hbm,
    out,
    bg,
    jitter,
    readings,
    noise,
    location,
    coupling,
    taper,
    rows_f32,
    send1,
    recv1,
    mem_f32,
    tiles,
    prior_all,
    dev,
    shared,
    prod,
    inc_f32,
    send2,
    recv2,
    bg_sem,
    load_sem,
    send1_sem,
    recv1_sem,
    sendp_sem,
    recvp_sem,
    send2_sem,
    recv2_sem,
):
    own = bg.shape[0]
    span = bg.shape[1] // slabs
    cols = span // LANES
    rows = own * cols
    members = own * slabs
    half = members // 2
    chunks = location.shape[1] // LANES
    links, blocks = coupling.shape
    bundles = members // 8
    per = slabs // bundles
    part_cols = cols // parts
    part_rows = own * part_cols
    me = lax.axis_index("slab")
    group = lax.axis_index("obs")
    home = me // per
    depth = bundles // 2

    def ahead(k):
        j = lax.rem(k + 2, bundles)
        z = lax.rem(home // 2 + depth - j // 2, depth)
        return z * 2 + lax.rem(home + j, 2)

    def behind(k):
        j = lax.rem(k + 2, bundles)
        z = lax.rem(home // 2 + j // 2, depth)
        return z * 2 + lax.rem(home + j, 2)

    barrier = pltpu.get_barrier_semaphore()

    @pl.loop(1, slabs)
    def _(k):
        pl.semaphore_signal(
            barrier, inc=1, device_id=(lax.rem(me + k, slabs), group), device_id_type=MESH
        )

    for k in range(1, groups):
        pl.semaphore_signal(
            barrier, inc=1, device_id=(me, lax.rem(group + k, groups)), device_id_type=MESH
        )

    def bg_load(v):
        at = pl.ds(pl.multiple_of(v * per * span, LANES), per * span)
        return pltpu.make_async_copy(bg_hbm.at[:, at], bg.at[:, at], bg_sem.at[v])

    @pl.loop(0, bundles)
    def _(k):
        bg_load(ahead(k)).start()

    loads = [
        pltpu.make_async_copy(source, target, load_sem.at[i])
        for i, (source, target) in enumerate(
            (
                (location_hbm, location),
                (jitter_hbm, jitter),
                (readings_hbm, readings),
                (noise_hbm, noise),
                (coupling_hbm, coupling),
                (taper_hbm, taper),
            )
        )
    ]
    for load in loads:
        load.start()

    def forward(to):
        return pltpu.make_async_remote_copy(
            src_ref=send1.at[to],
            dst_ref=recv1.at[me],
            send_sem=send1_sem.at[to],
            recv_sem=recv1_sem.at[me],
            device_id=(to, group),
            device_id_type=MESH,
        )

    def arriving(source):
        return pltpu.make_async_remote_copy(
            src_ref=send1.at[source],
            dst_ref=recv1.at[source],
            send_sem=send1_sem.at[source],
            recv_sem=recv1_sem.at[source],
            device_id=(source, group),
            device_id_type=MESH,
        )

    def pack(k):
        v = ahead(k)
        bg_load(v).wait()
        for j in range(per):
            s = v * per + j
            for q in range(cols):
                part = bg[:, pl.ds(pl.multiple_of(s * span + q * LANES, LANES), LANES)]
                if own == 1:
                    rows_f32[pl.ds(s * rows + q, 1), :] = part
                else:
                    rows_f32[pl.ds(s * rows + q, own, stride=cols), :] = part
            send1[s] = rows_f32[pl.ds(pl.multiple_of(s * rows, 16), rows), :].astype(jnp.bfloat16)

    def send(k):
        v = ahead(k)
        for j in range(per):
            to = v * per + j

            @pl.when(to != me)
            def _():
                forward(to).start()

    @pl.loop(0, bundles)
    def _(k):
        pack(k)

    pl.semaphore_wait(barrier, slabs - 1 + groups - 1)

    @pl.loop(0, bundles)
    def _(k):
        send(k)

    recv1[me] = send1[me]

    loads[0].wait()
    place = location[...]
    column = [
        jnp.broadcast_to(place[:, c * LANES : (c + 1) * LANES] >> 7, (8, LANES))
        for c in range(chunks)
    ]
    lane = [
        jnp.broadcast_to(place[:, c * LANES : (c + 1) * LANES] & (LANES - 1), (8, LANES))
        for c in range(chunks)
    ]

    @pl.loop(0, bundles)
    def _(k):
        v = behind(k)
        for j in range(per):
            source = v * per + j

            @pl.when(source != me)
            def _():
                arriving(source).wait_recv()

            mem_f32[pl.ds(pl.multiple_of(source * rows, 16), rows), :] = recv1[source].astype(
                jnp.float32
            )
        eight = pl.ds(pl.multiple_of(v * 8, 8), 8)
        values = [jnp.zeros((8, LANES), jnp.float32)] * chunks
        for q in range(cols):
            tile = mem_f32[pl.ds(v * 8 * cols + q, 8, stride=cols), :]
            tiles[q, eight, :] = tile
            for c in range(chunks):
                picked = jnp.take_along_axis(tile, lane[c], axis=1, mode="promise_in_bounds")
                values[c] = jnp.where(column[c] == q, picked, values[c])
        for c in range(chunks):
            prior_all[c, eight, :] = values[c]

    def share(c, to, owner):
        return pltpu.make_async_remote_copy(
            src_ref=shared.at[owner, c],
            dst_ref=shared.at[owner, c],
            send_sem=sendp_sem.at[to, c],
            recv_sem=recvp_sem.at[owner, c],
            device_id=(me, to),
            device_id_type=MESH,
        )

    for load in loads[1:]:
        load.wait()
    live = tally[0, 0]
    lanes = lax.broadcasted_iota(jnp.int32, (members, LANES), 1)
    for c in range(chunks):
        here = slice(c * LANES, (c + 1) * LANES)
        prior = prior_all[c]
        shift = prior - jnp.mean(prior, axis=0, keepdims=True)
        spread = jnp.sum(shift * shift, axis=0, keepdims=True) * (1.0 / (members - 1))
        innovation = (readings[:, here] + jitter[:, here].astype(jnp.float32) - prior) * (
            1.0 / (spread + noise[:, here])
        )
        gain = jnp.where(lanes + c * LANES < live, innovation, 0.0).astype(jnp.bfloat16)
        product = lax.dot_general(
            gain,
            shift.astype(jnp.bfloat16),
            (((1,), (1,)), ((), ())),
            preferred_element_type=jnp.float32,
        )
        packed = jnp.concatenate([product[:half], product[half:]], axis=1)
        prod[group * chunks + c] = packed
        shared[group, c] = packed.astype(jnp.bfloat16)
        for k in range(1, groups):
            share(c, lax.rem(group + k, groups), group).start()

    for q in range(cols):
        tile = tiles[q]
        dev[q] = (tile - jnp.mean(tile, axis=0, keepdims=True)).astype(jnp.bfloat16)

    for k in range(1, groups):
        source = lax.rem(group + k, groups)
        for c in range(chunks):
            share(c, source, source).wait_recv()
            prod[source * chunks + c] = shared[source, c].astype(jnp.float32)

    low_lane = lax.broadcasted_iota(jnp.int32, (2 * half, LANES), 1) < LANES // 2
    low_half = lax.broadcasted_iota(jnp.int32, (half, LANES), 1) < LANES // 2

    def backward(h, to):
        return pltpu.make_async_remote_copy(
            src_ref=send2.at[h, to],
            dst_ref=recv2.at[h, me],
            send_sem=send2_sem.at[h, to],
            recv_sem=recv2_sem.at[h, me],
            device_id=(to, group),
            device_id_type=MESH,
        )

    def back(h, source):
        return pltpu.make_async_remote_copy(
            src_ref=send2.at[h, source],
            dst_ref=recv2.at[h, source],
            send_sem=send2_sem.at[h, source],
            recv_sem=recv2_sem.at[h, source],
            device_id=(source, group),
            device_id_type=MESH,
        )

    for h in range(parts):
        for i in range(part_cols):
            q = h * part_cols + i
            pair = []
            for b in (2 * q, 2 * q + 1):
                total = taper[0, b] * prod[coupling[0, b]]
                for l in range(1, links):
                    total = total + taper[l, b] * prod[coupling[l, b]]
                pair.append(total * (1.0 / (members - 1)))
            pair = jnp.concatenate(pair, axis=0)
            left = jnp.concatenate(
                [jnp.where(low_lane, pair, 0.0), jnp.where(low_lane, 0.0, pair)], axis=0
            ).astype(jnp.bfloat16)
            right = dev[q]
            right = jnp.concatenate([right, right], axis=0)
            update = jnp.dot(left, right, preferred_element_type=jnp.float32)
            inc_f32[h, pl.ds(i, half, stride=part_cols), :] = jnp.where(
                low_half, update[:half], update[half : 2 * half]
            )
            inc_f32[h, pl.ds(i + half * part_cols, half, stride=part_cols), :] = jnp.where(
                low_half, update[2 * half : 3 * half], update[3 * half :]
            )

        @pl.loop(0, bundles)
        def _(k):
            for j in range(per):
                to = ahead(k) * per + j
                send2[h, to] = inc_f32[
                    h, pl.ds(pl.multiple_of(to * part_rows, 16), part_rows), :
                ].astype(jnp.bfloat16)

                @pl.when(to != me)
                def _():
                    backward(h, to).start()

    def finish(h, s, low):
        base = s * rows + h * part_rows
        rows_f32[pl.ds(pl.multiple_of(base, 16), part_rows), :] = low.astype(jnp.float32)
        for i in range(part_cols):
            q = h * part_cols + i
            at = pl.ds(pl.multiple_of(s * span + q * LANES, LANES), LANES)
            if own == 1:
                part = rows_f32[pl.ds(base + i, 1), :]
            else:
                part = rows_f32[pl.ds(base + i, own, stride=part_cols), :]
            out[:, at] = bg[:, at] + part

    for h in range(parts):
        recv2[h, me] = send2[h, me]

        @pl.loop(0, bundles)
        def _(k):
            for j in range(per):
                source = behind(k) * per + j

                @pl.when(source != me)
                def _():
                    back(h, source).wait_recv()

                finish(h, source, recv2[h, source])

    @pl.loop(1, slabs)
    def _(k):
        to = lax.rem(me + k, slabs)
        forward(to).wait_send()
        for h in range(parts):
            backward(h, to).wait_send()

    for k in range(1, groups):
        to = lax.rem(group + k, groups)
        for c in range(chunks):
            share(c, to, group).wait_send()


def solution(mesh):
    slabs, groups = mesh.shape["slab"], mesh.shape["obs"]

    def local(
        background_members,
        measurement_jitter,
        measurement_readings,
        measurement_noise_spread,
        measurement_grid_location,
        active_tallies,
        coupling_listing,
        taper_factors,
    ):
        own, points = background_members.shape
        span = points // slabs
        cols = span // LANES
        rows = own * cols
        members = own * slabs
        slots = measurement_grid_location.shape[1]
        chunks = slots // LANES
        blocks, links = coupling_listing.shape[1:]
        parts = 4 if rows % 64 == 0 else 1
        smem = pl.BlockSpec(memory_space=pltpu.SMEM)
        hbm = pl.BlockSpec(memory_space=pl.ANY)
        f32, bf16, i32 = jnp.float32, jnp.bfloat16, jnp.int32
        return pl.pallas_call(
            functools.partial(kernel, slabs, groups, parts),
            out_shape=pltpu.VMEM((own, points), f32),
            in_specs=[hbm] * 5 + [smem] + [hbm] * 2,
            out_specs=pl.BlockSpec(memory_space=pltpu.VMEM),
            scratch_shapes=[
                pltpu.VMEM((own, points), f32),
                pltpu.VMEM((members, slots), bf16),
                pltpu.VMEM((1, slots), f32),
                pltpu.VMEM((1, slots), f32),
                pltpu.VMEM((1, slots), i32),
                pltpu.SMEM((links, blocks), i32),
                pltpu.SMEM((links, blocks), f32),
                pltpu.VMEM((slabs * rows, LANES), f32),
                pltpu.VMEM((slabs, rows, LANES), bf16),
                pltpu.VMEM((slabs, rows, LANES), bf16),
                pltpu.VMEM((slabs * rows, LANES), f32),
                pltpu.VMEM((cols, members, LANES), f32),
                pltpu.VMEM((chunks, members, LANES), f32),
                pltpu.VMEM((cols, members, LANES), bf16),
                pltpu.VMEM((groups, chunks, members // 2, LANES), bf16),
                pltpu.VMEM((groups * chunks, members // 2, LANES), f32),
                pltpu.VMEM((parts, slabs * rows // parts, LANES), f32),
                pltpu.VMEM((parts, slabs, rows // parts, LANES), bf16),
                pltpu.VMEM((parts, slabs, rows // parts, LANES), bf16),
                pltpu.SemaphoreType.DMA((members // 8,)),
                pltpu.SemaphoreType.DMA((6,)),
                pltpu.SemaphoreType.DMA((slabs,)),
                pltpu.SemaphoreType.DMA((slabs,)),
                pltpu.SemaphoreType.DMA((groups, chunks)),
                pltpu.SemaphoreType.DMA((groups, chunks)),
                pltpu.SemaphoreType.DMA((parts, slabs)),
                pltpu.SemaphoreType.DMA((parts, slabs)),
            ],
            compiler_params=pltpu.CompilerParams(
                collective_id=0, has_side_effects=True, vmem_limit_bytes=60 * 1024 * 1024
            ),
            cost_estimate=pl.CostEstimate(
                flops=200_000_000, bytes_accessed=2_000_000, transcendentals=0
            ),
        )(
            background_members,
            measurement_jitter[:, 0, :],
            measurement_readings,
            measurement_noise_spread,
            measurement_grid_location,
            active_tallies,
            coupling_listing[0].T,
            taper_factors[0].T,
        )

    return jax.shard_map(
        local,
        mesh=mesh,
        in_specs=(
            P("slab", "obs"),
            P(None, "obs", "slab"),
            P("obs", "slab"),
            P("obs", "slab"),
            P("obs", "slab"),
            P("obs", "slab"),
            P("obs", "slab", None),
            P("obs", "slab", None),
        ),
        out_specs=P("slab", "obs"),
        check_vma=False,
    )
```

```python
import functools

import jax
import jax.numpy as jnp
from jax import lax
from jax.experimental import pallas as pl
from jax.experimental.pallas import tpu as pltpu
from jax.sharding import PartitionSpec as P

LANES = 128
MESH = pl.DeviceIdType.MESH


def kernel(
    slabs,
    groups,
    parts,
    bg_hbm,
    jitter_hbm,
    readings_hbm,
    noise_hbm,
    location_hbm,
    tally,
    coupling_hbm,
    taper_hbm,
    out,
    bg,
    jitter,
    readings,
    noise,
    location,
    coupling,
    taper,
    rows_f32,
    send1,
    recv1,
    mem_f32,
    tiles,
    prior_all,
    dev,
    shared,
    prod,
    inc_f32,
    send2,
    recv2,
    bg_sem,
    load_sem,
    send1_sem,
    recv1_sem,
    sendp_sem,
    recvp_sem,
    send2_sem,
    recv2_sem,
):
    own = bg.shape[0]
    span = bg.shape[1] // slabs
    cols = span // LANES
    rows = own * cols
    members = own * slabs
    half = members // 2
    chunks = location.shape[1] // LANES
    links, blocks = coupling.shape
    bundles = members // 8
    per = slabs // bundles
    part_cols = cols // parts
    part_rows = own * part_cols
    me = lax.axis_index("slab")
    group = lax.axis_index("obs")
    home = me // per
    depth = bundles // 2

    def ahead(k):
        j = lax.rem(k + 2, bundles)
        z = lax.rem(home // 2 + depth - j // 2, depth)
        return z * 2 + lax.rem(home + j, 2)

    def behind(k):
        j = lax.rem(k + 2, bundles)
        z = lax.rem(home // 2 + j // 2, depth)
        return z * 2 + lax.rem(home + j, 2)

    barrier = pltpu.get_barrier_semaphore()

    @pl.loop(1, slabs)
    def _(k):
        pl.semaphore_signal(
            barrier, inc=1, device_id=(lax.rem(me + k, slabs), group), device_id_type=MESH
        )

    for k in range(1, groups):
        pl.semaphore_signal(
            barrier, inc=1, device_id=(me, lax.rem(group + k, groups)), device_id_type=MESH
        )

    def bg_load(v):
        at = pl.ds(pl.multiple_of(v * per * span, LANES), per * span)
        return pltpu.make_async_copy(bg_hbm.at[:, at], bg.at[:, at], bg_sem.at[v])

    @pl.loop(0, bundles)
    def _(k):
        bg_load(ahead(k)).start()

    loads = [
        pltpu.make_async_copy(source, target, load_sem.at[i])
        for i, (source, target) in enumerate(
            (
                (location_hbm, location),
                (jitter_hbm, jitter),
                (readings_hbm, readings),
                (noise_hbm, noise),
                (coupling_hbm, coupling),
                (taper_hbm, taper),
            )
        )
    ]
    for load in loads:
        load.start()

    def forward(to):
        return pltpu.make_async_remote_copy(
            src_ref=send1.at[to],
            dst_ref=recv1.at[me],
            send_sem=send1_sem.at[to],
            recv_sem=recv1_sem.at[me],
            device_id=(to, group),
            device_id_type=MESH,
        )

    def arriving(source):
        return pltpu.make_async_remote_copy(
            src_ref=send1.at[source],
            dst_ref=recv1.at[source],
            send_sem=send1_sem.at[source],
            recv_sem=recv1_sem.at[source],
            device_id=(source, group),
            device_id_type=MESH,
        )

    def pack(k):
        v = ahead(k)
        bg_load(v).wait()
        for j in range(per):
            s = v * per + j
            for q in range(cols):
                part = bg[:, pl.ds(pl.multiple_of(s * span + q * LANES, LANES), LANES)]
                if own == 1:
                    rows_f32[pl.ds(s * rows + q, 1), :] = part
                else:
                    rows_f32[pl.ds(s * rows + q, own, stride=cols), :] = part
            send1[s] = rows_f32[pl.ds(pl.multiple_of(s * rows, 16), rows), :].astype(jnp.bfloat16)

    def send(k):
        v = ahead(k)
        for j in range(per):
            to = v * per + j

            @pl.when(to != me)
            def _():
                forward(to).start()

    @pl.loop(0, bundles)
    def _(k):
        pack(k)

    pl.semaphore_wait(barrier, slabs - 1 + groups - 1)

    @pl.loop(0, bundles)
    def _(k):
        send(k)

    recv1[me] = send1[me]

    loads[0].wait()
    place = location[...]
    column = [
        jnp.broadcast_to(place[:, c * LANES : (c + 1) * LANES] >> 7, (8, LANES))
        for c in range(chunks)
    ]
    lane = [
        jnp.broadcast_to(place[:, c * LANES : (c + 1) * LANES] & (LANES - 1), (8, LANES))
        for c in range(chunks)
    ]

    @pl.loop(0, bundles)
    def _(k):
        v = behind(k)
        for j in range(per):
            source = v * per + j

            @pl.when(source != me)
            def _():
                arriving(source).wait_recv()

            mem_f32[pl.ds(pl.multiple_of(source * rows, 16), rows), :] = recv1[source].astype(
                jnp.float32
            )
        eight = pl.ds(pl.multiple_of(v * 8, 8), 8)
        values = [jnp.zeros((8, LANES), jnp.float32)] * chunks
        for q in range(cols):
            tile = mem_f32[pl.ds(v * 8 * cols + q, 8, stride=cols), :]
            tiles[q, eight, :] = tile
            for c in range(chunks):
                picked = jnp.take_along_axis(tile, lane[c], axis=1, mode="promise_in_bounds")
                values[c] = jnp.where(column[c] == q, picked, values[c])
        for c in range(chunks):
            prior_all[c, eight, :] = values[c]

    def share(c, to, owner):
        return pltpu.make_async_remote_copy(
            src_ref=shared.at[owner, c],
            dst_ref=shared.at[owner, c],
            send_sem=sendp_sem.at[to, c],
            recv_sem=recvp_sem.at[owner, c],
            device_id=(me, to),
            device_id_type=MESH,
        )

    for load in loads[1:]:
        load.wait()
    live = tally[0, 0]
    lanes = lax.broadcasted_iota(jnp.int32, (members, LANES), 1)
    for c in range(chunks):
        here = slice(c * LANES, (c + 1) * LANES)
        prior = prior_all[c]
        shift = prior - jnp.mean(prior, axis=0, keepdims=True)
        spread = jnp.sum(shift * shift, axis=0, keepdims=True) * (1.0 / (members - 1))
        innovation = (readings[:, here] + jitter[:, here].astype(jnp.float32) - prior) * (
            1.0 / (spread + noise[:, here])
        )
        gain = jnp.where(lanes + c * LANES < live, innovation, 0.0).astype(jnp.bfloat16)
        product = lax.dot_general(
            gain,
            shift.astype(jnp.bfloat16),
            (((1,), (1,)), ((), ())),
            preferred_element_type=jnp.float32,
        )
        packed = jnp.concatenate([product[:half], product[half:]], axis=1)
        prod[group * chunks + c] = packed
        shared[group, c] = packed.astype(jnp.bfloat16)
        for k in range(1, groups):
            share(c, lax.rem(group + k, groups), group).start()

    for q in range(cols):
        tile = tiles[q]
        dev[q] = (tile - jnp.mean(tile, axis=0, keepdims=True)).astype(jnp.bfloat16)

    for k in range(1, groups):
        source = lax.rem(group + k, groups)
        for c in range(chunks):
            share(c, source, source).wait_recv()
            prod[source * chunks + c] = shared[source, c].astype(jnp.float32)

    low_lane = lax.broadcasted_iota(jnp.int32, (2 * half, LANES), 1) < LANES // 2
    low_half = lax.broadcasted_iota(jnp.int32, (half, LANES), 1) < LANES // 2

    def backward(h, to):
        return pltpu.make_async_remote_copy(
            src_ref=send2.at[h, to],
            dst_ref=recv2.at[h, me],
            send_sem=send2_sem.at[h, to],
            recv_sem=recv2_sem.at[h, me],
            device_id=(to, group),
            device_id_type=MESH,
        )

    def back(h, source):
        return pltpu.make_async_remote_copy(
            src_ref=send2.at[h, source],
            dst_ref=recv2.at[h, source],
            send_sem=send2_sem.at[h, source],
            recv_sem=recv2_sem.at[h, source],
            device_id=(source, group),
            device_id_type=MESH,
        )

    for h in range(parts):
        for i in range(part_cols):
            q = h * part_cols + i
            pair = []
            for b in (2 * q, 2 * q + 1):
                total = taper[0, b] * prod[coupling[0, b]]
                for l in range(1, links):
                    total = total + taper[l, b] * prod[coupling[l, b]]
                pair.append(total * (1.0 / (members - 1)))
            pair = jnp.concatenate(pair, axis=0)
            left = jnp.concatenate(
                [jnp.where(low_lane, pair, 0.0), jnp.where(low_lane, 0.0, pair)], axis=0
            ).astype(jnp.bfloat16)
            right = dev[q]
            right = jnp.concatenate([right, right], axis=0)
            update = jnp.dot(left, right, preferred_element_type=jnp.float32)
            inc_f32[h, pl.ds(i, half, stride=part_cols), :] = jnp.where(
                low_half, update[:half], update[half : 2 * half]
            )
            inc_f32[h, pl.ds(i + half * part_cols, half, stride=part_cols), :] = jnp.where(
                low_half, update[2 * half : 3 * half], update[3 * half :]
            )

        @pl.loop(0, bundles)
        def _(k):
            for j in range(per):
                to = ahead(k) * per + j
                send2[h, to] = inc_f32[
                    h, pl.ds(pl.multiple_of(to * part_rows, 16), part_rows), :
                ].astype(jnp.bfloat16)

                @pl.when(to != me)
                def _():
                    backward(h, to).start()

    def finish(h, s, low):
        base = s * rows + h * part_rows
        rows_f32[pl.ds(pl.multiple_of(base, 16), part_rows), :] = low.astype(jnp.float32)
        for i in range(part_cols):
            q = h * part_cols + i
            at = pl.ds(pl.multiple_of(s * span + q * LANES, LANES), LANES)
            if own == 1:
                part = rows_f32[pl.ds(base + i, 1), :]
            else:
                part = rows_f32[pl.ds(base + i, own, stride=part_cols), :]
            out[:, at] = bg[:, at] + part

    for h in range(parts):
        recv2[h, me] = send2[h, me]

        @pl.loop(0, bundles)
        def _(k):
            for j in range(per):
                source = behind(k) * per + j

                @pl.when(source != me)
                def _():
                    back(h, source).wait_recv()

                finish(h, source, recv2[h, source])

    @pl.loop(1, slabs)
    def _(k):
        to = lax.rem(me + k, slabs)
        forward(to).wait_send()
        for h in range(parts):
            backward(h, to).wait_send()

    for k in range(1, groups):
        to = lax.rem(group + k, groups)
        for c in range(chunks):
            share(c, to, group).wait_send()


def solution(mesh):
    slabs, groups = mesh.shape["slab"], mesh.shape["obs"]

    def local(
        background_members,
        measurement_jitter,
        measurement_readings,
        measurement_noise_spread,
        measurement_grid_location,
        active_tallies,
        coupling_listing,
        taper_factors,
    ):
        own, points = background_members.shape
        span = points // slabs
        cols = span // LANES
        rows = own * cols
        members = own * slabs
        slots = measurement_grid_location.shape[1]
        chunks = slots // LANES
        blocks, links = coupling_listing.shape[1:]
        parts = 1
        smem = pl.BlockSpec(memory_space=pltpu.SMEM)
        hbm = pl.BlockSpec(memory_space=pl.ANY)
        f32, bf16, i32 = jnp.float32, jnp.bfloat16, jnp.int32
        return pl.pallas_call(
            functools.partial(kernel, slabs, groups, parts),
            out_shape=pltpu.VMEM((own, points), f32),
            in_specs=[hbm] * 5 + [smem] + [hbm] * 2,
            out_specs=pl.BlockSpec(memory_space=pltpu.VMEM),
            scratch_shapes=[
                pltpu.VMEM((own, points), f32),
                pltpu.VMEM((members, slots), bf16),
                pltpu.VMEM((1, slots), f32),
                pltpu.VMEM((1, slots), f32),
                pltpu.VMEM((1, slots), i32),
                pltpu.SMEM((links, blocks), i32),
                pltpu.SMEM((links, blocks), f32),
                pltpu.VMEM((slabs * rows, LANES), f32),
                pltpu.VMEM((slabs, rows, LANES), bf16),
                pltpu.VMEM((slabs, rows, LANES), bf16),
                pltpu.VMEM((slabs * rows, LANES), f32),
                pltpu.VMEM((cols, members, LANES), f32),
                pltpu.VMEM((chunks, members, LANES), f32),
                pltpu.VMEM((cols, members, LANES), bf16),
                pltpu.VMEM((groups, chunks, members // 2, LANES), bf16),
                pltpu.VMEM((groups * chunks, members // 2, LANES), f32),
                pltpu.VMEM((parts, slabs * rows // parts, LANES), f32),
                pltpu.VMEM((parts, slabs, rows // parts, LANES), bf16),
                pltpu.VMEM((parts, slabs, rows // parts, LANES), bf16),
                pltpu.SemaphoreType.DMA((members // 8,)),
                pltpu.SemaphoreType.DMA((6,)),
                pltpu.SemaphoreType.DMA((slabs,)),
                pltpu.SemaphoreType.DMA((slabs,)),
                pltpu.SemaphoreType.DMA((groups, chunks)),
                pltpu.SemaphoreType.DMA((groups, chunks)),
                pltpu.SemaphoreType.DMA((parts, slabs)),
                pltpu.SemaphoreType.DMA((parts, slabs)),
            ],
            compiler_params=pltpu.CompilerParams(
                collective_id=0, has_side_effects=True, vmem_limit_bytes=60 * 1024 * 1024
            ),
            cost_estimate=pl.CostEstimate(
                flops=200_000_000, bytes_accessed=2_000_000, transcendentals=0
            ),
        )(
            background_members,
            measurement_jitter[:, 0, :],
            measurement_readings,
            measurement_noise_spread,
            measurement_grid_location,
            active_tallies,
            coupling_listing[0].T,
            taper_factors[0].T,
        )

    return jax.shard_map(
        local,
        mesh=mesh,
        in_specs=(
            P("slab", "obs"),
            P(None, "obs", "slab"),
            P("obs", "slab"),
            P("obs", "slab"),
            P("obs", "slab"),
            P("obs", "slab"),
            P("obs", "slab", None),
            P("obs", "slab", None),
        ),
        out_specs=P("slab", "obs"),
        check_vma=False,
    )
```
